128 devices in a mesh: seq: 16 (over z, x), chan: 8 (over y, core).
Axes of the slice: x: 4, y: 4, z: 4, core: 2. Of those that a mesh axis runs over, the one named last changes fastest.
Arguments:
- hidden_in: bfloat16 [32768, 8192], P('seq', 'chan'), may hold values from -6 to 6
- projection: bfloat16 [3, 8192, 512], P(None, 'chan'), may hold values from -0.0625 to 0.0625
- filter_taps: bfloat16 [512, 32768], P('chan', 'seq'), may hold values from -1.1 to 1.1
Outputs:
- gated: bfloat16 [512, 32768], P('chan', 'seq')
The draws below stay inside these ranges and needn't reach their ends.
All inputs are finite; a program needn't handle non-finite values.
Results may differ from the reference program's by a relative error of at most 0.007.
Values may be sent and summed in bfloat16 or wider, within the bound.
A program may use at most 128 MiB of HBM per device.

```python
import math
import jax
import jax.numpy as jnp

D = 8192
CHANNELS = 512
TOKENS = 32768


def draw_filter_taps(key, part):
    key = jax.random.fold_in(key, 11)
    keys = jax.random.split(key, 6)
    genomic_coordinate = jnp.arange(TOKENS, dtype=jnp.float32)
    pick = jax.random.uniform(keys[0], (CHANNELS, 1))
    fast_share = 0.5
    noise_perturbation = jax.random.truncated_normal(keys[1], -4.0, 4.0, (CHANNELS, TOKENS))
    fast_reach = jnp.exp(jax.random.uniform(keys[2], (CHANNELS, 1), minval=math.log(30.0), maxval=math.log(50.0)))
    slow_reach = jnp.exp(jax.random.uniform(keys[3], (CHANNELS, 1), minval=math.log(float(TOKENS)), maxval=math.log(4.0 * TOKENS)))
    kernel_span = jnp.where(pick < fast_share, fast_reach, slow_reach)
    flagged_indices = jax.random.randint(keys[4], (3, 1), 1, TOKENS).astype(jnp.float32)
    missing_readings = jax.random.uniform(keys[5], (3, 1), minval=0.5, maxval=0.8)
    spike_occurrences = jnp.prod(jnp.where(genomic_coordinate[None, :] >= flagged_indices, missing_readings, 1.0), axis=0)
    multiplier_coefficient = jnp.sqrt(2.0 / jnp.minimum(kernel_span, float(TOKENS)))
    return (noise_perturbation * multiplier_coefficient * jnp.exp(-genomic_coordinate[None, :] / kernel_span) * spike_occurrences[None, :]).astype(jnp.bfloat16)


def shard_levels(own_key, shape, pieces, least, top_value):
    factor_of, own = 1.0, jax.random.fold_in(own_key, 6)
    for position, blocks in pieces:
        draws = jnp.exp(jax.random.uniform(jax.random.fold_in(own, position), (blocks,), jnp.float32, least / len(pieces), top_value / len(pieces)))
        factor_of = factor_of * jnp.repeat(draws, shape[position] // blocks).reshape([-1 if axis == position else 1 for axis in range(len(shape))])
    return factor_of


def gaussian(own_key, shape, width, bound, pieces=(), kind=jnp.bfloat16):
    drawn = width * jax.random.normal(own_key, shape, jnp.float32)
    if pieces:
        drawn = drawn * shard_levels(own_key, shape, pieces, -0.22, 0.18)
    return jnp.clip(drawn, -bound, bound).astype(kind)


def setup_inputs(seed: int = 0) -> dict:
    streams_of = jax.random.split(jax.random.key(seed), 4)
    return {
        "hidden_in": gaussian(streams_of[0], (TOKENS, D), 1.0, 6.0, ((0, 16), (1, 8))),
        "projection": gaussian(streams_of[1], (3, D, CHANNELS), D ** -0.5, 0.0625, ((1, 8),)),
        "filter_taps": draw_filter_taps(jax.random.fold_in(streams_of[3], 71), 0),
    }


def reference(hidden_in, projection, filter_taps):
    rows = []
    for index in range(3):
        part_value = jnp.dot(hidden_in, projection[index], preferred_element_type=jnp.float32)
        rows.append(part_value.astype(jnp.bfloat16).T)
    gating, key_part, value_part = rows
    mixed = (key_part.astype(jnp.float32) * value_part.astype(jnp.float32)).astype(jnp.bfloat16)
    length = mixed.shape[1]
    spectra = jnp.fft.rfft(mixed.astype(jnp.float32), n=2 * length, axis=1)
    spectra = spectra * jnp.fft.rfft(filter_taps.astype(jnp.float32), n=2 * length, axis=1)
    convolved = jnp.fft.irfft(spectra, n=2 * length, axis=1)[:, :length]
    return (gating.astype(jnp.float32) * convolved).astype(jnp.bfloat16)
```

```python
import jax
import jax.numpy as jnp
import numpy as np
from jax import lax
from jax.sharding import PartitionSpec as P

ROWS, COLS = 256, 128
HIGH = lax.Precision.HIGH


def transform_tables():
    total = ROWS * COLS
    counter = np.arange(ROWS)
    first = 2.0 * np.pi * ((counter[:, None] * (4 * counter[None, :] + 1)) % (4 * ROWS)) / (4 * ROWS)
    inner = np.arange(COLS)
    twist = 2.0 * np.pi * (inner[None, :] * (4 * counter[:, None] + 1)) / (4 * total)
    second = 2.0 * np.pi * ((inner[:, None] * inner[None, :]) % COLS) / COLS
    return first, twist, second


def forward(signal, tables):
    first, twist, second = tables
    cos1, sin1 = np.float32(np.cos(first.T)), np.float32(np.sin(first.T))
    cosw, sinw = np.float32(np.cos(twist)), np.float32(np.sin(twist))
    cos2, sin2 = np.float32(np.cos(second)), np.float32(np.sin(second))
    real = jnp.einsum("kj,cjb->ckb", cos1, signal, precision=HIGH)
    imag = -jnp.einsum("kj,cjb->ckb", sin1, signal, precision=HIGH)
    real, imag = real * cosw + imag * sinw, imag * cosw - real * sinw
    both = jnp.concatenate([real, imag], axis=-1)
    mix = np.block([[cos2, -sin2], [sin2, cos2]])
    both = jnp.einsum("ckb,bl->ckl", both, mix, precision=HIGH)
    return both[..., :COLS], both[..., COLS:]


def backward(real, imag, tables):
    first, twist, second = tables
    cosw, sinw = np.float32(np.cos(twist)), np.float32(np.sin(twist))
    cos2, sin2 = np.float32(np.cos(second)), np.float32(np.sin(second))
    both = jnp.concatenate([real, imag], axis=-1)
    mix = np.block([[cos2, sin2], [-sin2, cos2]])
    both = jnp.einsum("ckb,bl->ckl", both, mix, precision=HIGH)
    real, imag = both[..., :COLS], both[..., COLS:]
    real, imag = real * cosw - imag * sinw, imag * cosw + real * sinw
    both = jnp.concatenate([real, imag], axis=1)
    last = np.float32(np.concatenate([np.cos(first), -np.sin(first)], axis=1) / (ROWS * COLS))
    return jnp.einsum("jk,ckb->cjb", last, both, precision=HIGH)


def to_channels(block):
    blocks = lax.axis_size("seq")
    block = block.reshape(blocks, -1, block.shape[-1])
    moved = lax.all_to_all(block, "seq", 0, 0, tiled=False)
    moved = jnp.swapaxes(moved, 0, 1)
    return moved.reshape(moved.shape[0], ROWS, COLS)


def to_positions(whole):
    blocks = lax.axis_size("seq")
    whole = whole.reshape(whole.shape[0], blocks, -1)
    moved = lax.all_to_all(jnp.swapaxes(whole, 0, 1), "seq", 0, 0, tiled=False)
    return moved.reshape(-1, moved.shape[-1])


def per_device(hidden_in, projection, filter_taps):
    tables = transform_tables()
    taps = to_channels(filter_taps).astype(jnp.float32)
    filter_real, filter_imag = forward(taps, tables)
    projected = lax.psum_scatter(
        jnp.einsum("td,jdc->cjt", hidden_in, projection, preferred_element_type=jnp.float32),
        "chan",
        scatter_dimension=0,
        tiled=True,
    ).astype(jnp.bfloat16)
    gating = projected[:, 0]
    mixed = (projected[:, 1].astype(jnp.float32) * projected[:, 2].astype(jnp.float32)).astype(
        jnp.bfloat16
    )
    real, imag = forward(to_channels(mixed).astype(jnp.float32), tables)
    real, imag = (
        real * filter_real - imag * filter_imag,
        real * filter_imag + imag * filter_real,
    )
    convolved = to_positions(backward(real, imag, tables))
    return (gating.astype(jnp.float32) * convolved).astype(jnp.bfloat16)


def solution(mesh):
    placed = (P("seq", "chan"), P(None, "chan", None), P("chan", "seq"))
    return jax.shard_map(
        per_device, mesh=mesh, in_specs=placed, out_specs=P("chan", "seq"), check_vma=False
    )
```

```python
import functools

import jax
import jax.numpy as jnp
import numpy as np
from jax import lax
from jax.experimental import pallas as pl
from jax.experimental.pallas import tpu as pltpu
from jax.sharding import PartitionSpec as P

ROWS, COLS = 256, 128
CHUNKS = 6
MIXES = 4
HALF = 1024
TILE = 256
BF16 = jnp.bfloat16
F32 = jnp.float32


def split_table(table):
    high = np.asarray(table, np.float32).astype(BF16)
    low = (np.asarray(table, np.float64) - high.astype(np.float64)).astype(np.float32).astype(BF16)
    return np.stack([high, low])


def transform_tables():
    total = ROWS * COLS
    counter = np.arange(ROWS)
    outer = 2.0 * np.pi * ((counter[:, None] * (4 * counter[None, :] + 1)) % (4 * ROWS)) / (4 * ROWS)
    inner = np.arange(COLS)
    twist = 2.0 * np.pi * (inner[None, :] * (4 * counter[:, None] + 1)) / (4 * total)
    second = 2.0 * np.pi * ((inner[:, None] * inner[None, :]) % COLS) / COLS
    first = np.concatenate([np.cos(outer.T), -np.sin(outer.T)], axis=0)
    last = np.concatenate([np.cos(outer), -np.sin(outer)], axis=1) / total
    cos2, sin2 = np.cos(second), np.sin(second)
    ahead = np.block([[cos2, -sin2], [sin2, cos2]])
    back = np.block([[cos2, sin2], [-sin2, cos2]])
    turn = np.stack([np.cos(twist), -np.sin(twist)]).astype(np.float32)
    return (
        split_table(first),
        split_table(ahead),
        split_table(back),
        split_table(last),
        turn,
    )


def dot(left, right):
    return jnp.dot(left, right, preferred_element_type=F32)


def halves_of(value):
    high = value.astype(BF16)
    return high, (value - high.astype(F32)).astype(BF16)


def kernel(
    hidden_hbm, proj_hbm, taps_hbm, first_hbm, ahead_hbm, back_hbm, last_hbm, turn_hbm,
    out_hbm,
    hidden, proj, taps, first, ahead, back, last, turn,
    weights, own, core_out, core_in, ring_out, ring_in,
    relay, taps_out, taps_in, mixed_out, mixed_in, spectrum, conv_out, conv_in, gates, gated,
    load_sem, core_send, core_recv, ring_send, ring_recv,
    taps_send, taps_recv, mixed_send, mixed_recv, conv_send, conv_recv, store_sem,
):
    seq = lax.axis_index("seq")
    chan = lax.axis_index("chan")
    blocks = lax.axis_size("seq")
    y = chan // 2
    core = lax.rem(chan, 2)
    partner = {"chan": y * 2 + 1 - core}
    right = {"chan": lax.rem(y + 1, 4) * 2 + core}
    left = {"chan": lax.rem(y + 3, 4) * 2 + core}

    loads = []

    def load(src, dst):
        copy = pltpu.make_async_copy(src, dst, load_sem.at[len(loads)])
        copy.start()
        loads.append(copy)
        return copy

    proj_loads = [None, load(proj_hbm.at[1], proj.at[1]), load(proj_hbm.at[2], proj.at[2])]
    hidden_loads = [
        load(hidden_hbm.at[pl.ds(n * HALF, HALF)], hidden.at[pl.ds(n * HALF, HALF)])
        for n in range(2)
    ]
    taps_load = load(taps_hbm, taps)
    proj_loads[0] = load(proj_hbm.at[0], proj.at[0])
    table_loads = [
        load(first_hbm, first),
        load(ahead_hbm, ahead),
        load(back_hbm, back),
        load(last_hbm, last),
        load(turn_hbm, turn),
    ]

    barrier = pltpu.get_barrier_semaphore()
    for near in (partner, right, left):
        pl.semaphore_signal(barrier, inc=1, device_id=near, device_id_type=pl.DeviceIdType.MESH)

    @pl.loop(1, blocks)
    def _(step):
        pl.semaphore_signal(
            barrier,
            inc=1,
            device_id={"seq": lax.rem(seq + step, blocks)},
            device_id_type=pl.DeviceIdType.MESH,
        )

    def remote(src, dst, send, recv, device):
        return pltpu.make_async_remote_copy(
            src_ref=src, dst_ref=dst, send_sem=send, recv_sem=recv,
            device_id=device, device_id_type=pl.DeviceIdType.MESH,
        )

    def exchange(src, dst, send, recv):
        pltpu.make_async_copy(src.at[seq], dst.at[seq], recv).start()

        @pl.loop(1, blocks)
        def _(step):
            peer = lax.rem(seq + step, blocks)
            remote(src.at[peer], dst.at[seq], send, recv, {"seq": peer}).start()

    def exchange_arrived(src, dst, recv):
        pltpu.make_async_copy(src, dst, recv).wait()

    def exchange_left(src, dst, send):
        count = blocks - 1
        pltpu.make_async_copy(src.at[pl.ds(0, count)], dst.at[pl.ds(0, count)], send).wait()

    def spread(block, part):
        for tile in range(HALF // COLS):
            relay[pl.ds((part * (HALF // COLS) + tile) * 16, 16), :] = block[
                :, tile * COLS : (tile + 1) * COLS
            ]

    def turn_weights(kind):
        proj_loads[kind].wait()
        for ahead_by in range(4):
            lane = pl.multiple_of(lax.rem(y + ahead_by, 4) * 128, 128)
            turned = proj[kind, :, pl.ds(lane, 128)].T
            for side in range(2):
                place = (1 - core if side == 0 else core) * 128 + 32 * ahead_by
                if kind == 0:
                    for part in range(2):
                        row = pl.multiple_of(place, 32)
                        weights[MIXES + part, pl.ds(row, 32), :] = turned[
                            side * 64 + 32 * part : side * 64 + 32 * part + 32
                        ]
                else:
                    for part in range(MIXES):
                        row = pl.multiple_of(place + 16 * (kind - 1), 16)
                        weights[part, pl.ds(row, 16), :] = turned[
                            side * 64 + 16 * part : side * 64 + 16 * part + 16
                        ]

    def core_copy(c, h):
        return remote(
            core_out.at[c, h], core_in.at[c, h], core_send.at[c, h], core_recv.at[c, h], partner
        )

    def ring_copy(c, kind):
        return remote(
            ring_out.at[c, kind], ring_in.at[c, kind], ring_send.at[c, kind],
            ring_recv.at[c, kind], right if kind % 2 == 0 else left,
        )

    def multiply(c):
        for h in range(2):
            if c == 0:
                hidden_loads[h].wait()

            @pl.loop(0, HALF // TILE)
            def _(n):
                rows = pl.multiple_of(h * HALF + n * TILE, TILE)
                product = lax.dot_general(
                    weights[c], hidden[pl.ds(rows, TILE), :],
                    (((1,), (1,)), ((), ())), preferred_element_type=F32,
                )
                lanes = pl.ds(pl.multiple_of(n * TILE, TILE), TILE)
                core_out[c, h, :, lanes] = product[:128].astype(BF16)
                own[c, h, :, lanes] = product[128:]

            core_copy(c, h).start()

    def combine(c):
        for h in range(2):
            core_copy(c, h).wait_recv()
            ring_out[c, h] = (own[c, h, 64:96] + core_in[c, h, 64:96].astype(F32)).astype(BF16)
            ring_copy(c, h).start()
            direct, later = (96, 32) if h == 0 else (32, 96)
            kind = 3 if h == 0 else 2
            ring_out[c, kind] = (
                own[c, h, direct : direct + 32] + core_in[c, h, direct : direct + 32].astype(F32)
            ).astype(BF16)
            ring_copy(c, kind).start()
            for row in (0, later):
                own[c, h, row : row + 32] = own[c, h, row : row + 32] + core_in[
                    c, h, row : row + 32
                ].astype(F32)

    def pass_on(c):
        for h in range(2):
            ring_copy(c, h).wait_recv()
            later = 32 if h == 0 else 96
            ring_out[c, 4 + h] = (
                own[c, h, later : later + 32] + ring_in[c, h].astype(F32)
            ).astype(BF16)
            ring_copy(c, 4 + h).start()

    def finish(c):
        for h in range(2):
            kinds = (3, 4) if h == 0 else (2, 5)
            total = own[c, h, 0:32]
            for kind in kinds:
                ring_copy(c, kind).wait_recv()
                total = total + ring_in[c, kind].astype(F32)
            if c >= MIXES:
                gates[pl.ds((c - MIXES) * 32, 32), pl.ds(h * HALF, HALF)] = total
            else:
                spread(total[:16] * total[16:], h)
        if c < MIXES:
            for peer in range(16):
                mixed_out[c, peer] = relay[pl.ds(peer, 16, stride=16), :].astype(BF16)
            exchange(mixed_out.at[c], mixed_in.at[c], mixed_send.at[c], mixed_recv.at[c])

    def transformed(signal):
        value = dot(first[0], signal) + dot(first[1], signal)
        real, imag = value[:ROWS], value[ROWS:]
        value = jnp.concatenate(
            [real * turn[0] - imag * turn[1], real * turn[1] + imag * turn[0]], axis=1
        )
        high, low = halves_of(value)
        return dot(high, ahead[0]) + dot(high, ahead[1]) + dot(low, ahead[0])

    def send_taps():
        taps_load.wait()
        for q in range(MIXES):
            for h in range(2):
                spread(taps[q * 16 : q * 16 + 16, h * HALF : (h + 1) * HALF].astype(F32), h)
            for peer in range(16):
                taps_out[peer, q] = relay[pl.ds(peer, 16, stride=16), :].astype(BF16)
        exchange(taps_out, taps_in, taps_send, taps_recv)

    def filter_spectra():
        exchange_arrived(taps_out, taps_in, taps_recv)
        for copy in table_loads:
            copy.wait()
        for q in range(MIXES):
            spectrum[q] = transformed(taps_in[:, q].reshape(ROWS, COLS))

    def convolve(q):
        exchange_arrived(mixed_out.at[q], mixed_in.at[q], mixed_recv.at[q])
        value = transformed(mixed_in[q].reshape(ROWS, COLS))
        real, imag = value[:, :COLS], value[:, COLS:]
        freal, fimag = spectrum[q, :, :COLS], spectrum[q, :, COLS:]
        value = jnp.concatenate(
            [real * freal - imag * fimag, real * fimag + imag * freal], axis=1
        )
        high, low = halves_of(value)
        value = dot(high, back[0]) + dot(high, back[1]) + dot(low, back[0])
        real, imag = value[:, :COLS], value[:, COLS:]
        value = jnp.concatenate(
            [real * turn[0] + imag * turn[1], imag * turn[0] - real * turn[1]], axis=0
        )
        high, low = halves_of(value)
        value = dot(last[0], high) + dot(last[0], low) + dot(last[1], high)
        conv_out[q] = value.reshape(16, 16, COLS)
        exchange(conv_out.at[q], conv_in.at[q], conv_send.at[q], conv_recv.at[q])

    def emit(q):
        exchange_arrived(conv_out.at[q], conv_in.at[q], conv_recv.at[q])
        relay[...] = conv_in[q].reshape(256, COLS)
        rows = pl.ds(q * 16, 16)
        for tile in range(16):
            lanes = pl.ds(tile * COLS, COLS)
            part = relay[pl.ds(tile, 16, stride=16), :]
            gated[rows, lanes] = (gates[rows, lanes] * part).astype(BF16)
        pltpu.make_async_copy(gated.at[rows], out_hbm.at[rows], store_sem.at[q]).start()

    turn_weights(1)
    turn_weights(2)
    pl.semaphore_wait(barrier, 3 + blocks - 1)
    multiply(0)
    send_taps()
    multiply(1)
    combine(0)
    turn_weights(0)
    multiply(2)
    pass_on(0)
    combine(1)
    filter_spectra()
    finish(0)
    multiply(3)
    pass_on(1)
    combine(2)
    finish(1)
    convolve(0)
    multiply(4)
    pass_on(2)
    combine(3)
    finish(2)
    convolve(1)
    multiply(5)
    pass_on(3)
    combine(4)
    finish(3)
    convolve(2)
    pass_on(4)
    combine(5)
    finish(4)
    convolve(3)
    pass_on(5)
    emit(0)
    emit(1)
    finish(5)
    emit(2)
    emit(3)

    for c in range(CHUNKS):
        for h in range(2):
            core_copy(c, h).wait_send()
        for kind in range(6):
            ring_copy(c, kind).wait_send()
    exchange_left(taps_out, taps_in, taps_send)
    for q in range(MIXES):
        exchange_left(mixed_out.at[q], mixed_in.at[q], mixed_send.at[q])
        exchange_left(conv_out.at[q], conv_in.at[q], conv_send.at[q])
        rows = pl.ds(q * 16, 16)
        pltpu.make_async_copy(gated.at[rows], out_hbm.at[rows], store_sem.at[q]).wait()


def per_device(hidden_in, projection, filter_taps):
    tables = transform_tables()
    blocks = lax.axis_size("seq")
    anywhere = pl.BlockSpec(memory_space=pl.ANY)
    dma = pltpu.SemaphoreType.DMA
    return pl.pallas_call(
        kernel,
        out_shape=jax.ShapeDtypeStruct(filter_taps.shape, BF16),
        in_specs=[anywhere] * (3 + len(tables)),
        out_specs=anywhere,
        scratch_shapes=[
            pltpu.VMEM(hidden_in.shape, BF16),
            pltpu.VMEM(projection.shape, BF16),
            pltpu.VMEM(filter_taps.shape, BF16),
        ]
        + [pltpu.VMEM(table.shape, table.dtype) for table in tables]
        + [
            pltpu.VMEM((CHUNKS, 256, hidden_in.shape[1]), BF16),
            pltpu.VMEM((CHUNKS, 2, 128, HALF), F32),
            pltpu.VMEM((CHUNKS, 2, 128, HALF), BF16),
            pltpu.VMEM((CHUNKS, 2, 128, HALF), BF16),
            pltpu.VMEM((CHUNKS, 6, 32, HALF), BF16),
            pltpu.VMEM((CHUNKS, 6, 32, HALF), BF16),
            pltpu.VMEM((256, COLS), F32),
            pltpu.VMEM((blocks, MIXES, 16, COLS), BF16),
            pltpu.VMEM((blocks, MIXES, 16, COLS), BF16),
            pltpu.VMEM((MIXES, blocks, 16, COLS), BF16),
            pltpu.VMEM((MIXES, blocks, 16, COLS), BF16),
            pltpu.VMEM((MIXES, ROWS, 2 * COLS), F32),
            pltpu.VMEM((MIXES, blocks, 16, COLS), F32),
            pltpu.VMEM((MIXES, blocks, 16, COLS), F32),
            pltpu.VMEM(filter_taps.shape, F32),
            pltpu.VMEM(filter_taps.shape, BF16),
            dma((11,)),
            dma((CHUNKS, 2)),
            dma((CHUNKS, 2)),
            dma((CHUNKS, 6)),
            dma((CHUNKS, 6)),
            dma(()),
            dma(()),
            dma((MIXES,)),
            dma((MIXES,)),
            dma((MIXES,)),
            dma((MIXES,)),
            dma((MIXES,)),
        ],
        compiler_params=pltpu.CompilerParams(
            collective_id=0, has_side_effects=True, vmem_limit_bytes=60 * 1024 * 1024
        ),
        cost_estimate=pl.CostEstimate(
            flops=7_000_000_000, bytes_accessed=8_000_000, transcendentals=0
        ),
    )(hidden_in, projection, filter_taps, *[jnp.asarray(table) for table in tables])


def solution(mesh):
    placed = (P("seq", "chan"), P(None, "chan", None), P("chan", "seq"))
    return jax.shard_map(
        per_device, mesh=mesh, in_specs=placed, out_specs=P("chan", "seq"), check_vma=False
    )
```

```python
import functools

import jax
import jax.numpy as jnp
import numpy as np
from jax import lax
from jax.experimental import pallas as pl
from jax.experimental.pallas import tpu as pltpu
from jax.sharding import PartitionSpec as P

ROWS, COLS = 256, 128
CHUNKS = 6
MIXES = 4
HALF = 1024
TILE = 256
BF16 = jnp.bfloat16
F32 = jnp.float32


def split_table(table):
    high = np.asarray(table, np.float32).astype(BF16)
    low = (np.asarray(table, np.float64) - high.astype(np.float64)).astype(np.float32).astype(BF16)
    return np.stack([high, low])


def transform_tables():
    total = ROWS * COLS
    counter = np.arange(ROWS)
    outer = 2.0 * np.pi * ((counter[:, None] * (4 * counter[None, :] + 1)) % (4 * ROWS)) / (4 * ROWS)
    inner = np.arange(COLS)
    twist = 2.0 * np.pi * (inner[None, :] * (4 * counter[:, None] + 1)) / (4 * total)
    second = 2.0 * np.pi * ((inner[:, None] * inner[None, :]) % COLS) / COLS
    first = np.concatenate([np.cos(outer.T), -np.sin(outer.T)], axis=0)
    last = np.concatenate([np.cos(outer), -np.sin(outer)], axis=1) / total
    cos2, sin2 = np.cos(second), np.sin(second)
    ahead = np.block([[cos2, -sin2], [sin2, cos2]])
    back = np.block([[cos2, sin2], [-sin2, cos2]])
    turn = np.stack([np.cos(twist), -np.sin(twist)]).astype(np.float32)
    return (
        split_table(first),
        split_table(ahead),
        split_table(back),
        split_table(last),
        turn,
    )


def dot(left, right):
    return jnp.dot(left, right, preferred_element_type=F32)


def halves_of(value):
    high = value.astype(BF16)
    return high, (value - high.astype(F32)).astype(BF16)


def kernel(
    hidden_hbm, proj_hbm, taps_hbm, first_hbm, ahead_hbm, back_hbm, last_hbm, turn_hbm,
    out_hbm,
    hidden, proj, taps, first, ahead, back, last, turn,
    weights, own, core_out, core_in, ring_out, ring_in,
    relay, taps_out, taps_in, mixed_out, mixed_in, spectrum, conv_out, conv_in, gates, gated,
    load_sem, core_send, core_recv, ring_send, ring_recv,
    taps_send, taps_recv, mixed_send, mixed_recv, conv_send, conv_recv, store_sem, near_sem, far_sem,
):
    seq = lax.axis_index("seq")
    chan = lax.axis_index("chan")
    blocks = lax.axis_size("seq")
    y = chan // 2
    core = lax.rem(chan, 2)
    partner = {"chan": y * 2 + 1 - core}
    right = {"chan": lax.rem(y + 1, 4) * 2 + core}
    left = {"chan": lax.rem(y + 3, 4) * 2 + core}

    loads = []

    def load(src, dst):
        copy = pltpu.make_async_copy(src, dst, load_sem.at[len(loads)])
        copy.start()
        loads.append(copy)
        return copy

    proj_loads = [None, load(proj_hbm.at[1], proj.at[1]), load(proj_hbm.at[2], proj.at[2])]
    hidden_loads = [
        load(hidden_hbm.at[pl.ds(n * HALF, HALF)], hidden.at[pl.ds(n * HALF, HALF)])
        for n in range(2)
    ]
    taps_load = load(taps_hbm, taps)
    proj_loads[0] = load(proj_hbm.at[0], proj.at[0])
    table_loads = [
        load(first_hbm, first),
        load(ahead_hbm, ahead),
        load(back_hbm, back),
        load(last_hbm, last),
        load(turn_hbm, turn),
    ]

    def signal(semaphore, device):
        pl.semaphore_signal(
            semaphore, inc=1, device_id=device, device_id_type=pl.DeviceIdType.MESH
        )

    side = 4
    z, x = seq // side, lax.rem(seq, side)

    def plane(by_z, by_x):
        return {"seq": lax.rem(z + by_z, side) * side + lax.rem(x + by_x, side)}

    around = [plane(0, 1), plane(0, side - 1), plane(1, 0), plane(side - 1, 0)]
    across = [plane(0, 2), plane(2, 0)]
    barrier = pltpu.get_barrier_semaphore()
    for near in [partner, right, left] + around:
        signal(barrier, near)

    def remote(src, dst, send, recv, device):
        return pltpu.make_async_remote_copy(
            src_ref=src, dst_ref=dst, send_sem=send, recv_sem=recv,
            device_id=device, device_id_type=pl.DeviceIdType.MESH,
        )

    def exchange(src, dst, send, recv):
        pltpu.make_async_copy(src(seq), dst(seq), recv).start()

        @pl.loop(1, blocks)
        def _(step):
            peer = lax.rem(seq + step, blocks)
            remote(src(peer), dst(seq), send, recv, {"seq": peer}).start()

    def exchange_arrived(src, dst, recv):
        pltpu.make_async_copy(src, dst, recv).wait()

    def exchange_left(src, dst, send, count):
        pltpu.make_async_copy(src.at[pl.ds(0, count)], dst.at[pl.ds(0, count)], send).wait()

    def rows_of(ref):
        return lambda peer: ref.at[pl.ds(pl.multiple_of(peer * 16, 16), 16)]

    def spread(block, part):
        for tile in range(HALF // COLS):
            relay[pl.ds((part * (HALF // COLS) + tile) * 16, 16), :] = block[
                :, tile * COLS : (tile + 1) * COLS
            ]

    def turn_weights(kind):
        proj_loads[kind].wait()
        for ahead_by in range(4):
            lane = pl.multiple_of(lax.rem(y + ahead_by, 4) * 128, 128)
            turned = proj[kind, :, pl.ds(lane, 128)].T
            for side in range(2):
                place = (1 - core if side == 0 else core) * 128 + 32 * ahead_by
                if kind == 0:
                    for part in range(2):
                        row = pl.multiple_of(place, 32)
                        weights[MIXES + part, pl.ds(row, 32), :] = turned[
                            side * 64 + 32 * part : side * 64 + 32 * part + 32
                        ]
                else:
                    for part in range(MIXES):
                        row = pl.multiple_of(place + 16 * (kind - 1), 16)
                        weights[part, pl.ds(row, 16), :] = turned[
                            side * 64 + 16 * part : side * 64 + 16 * part + 16
                        ]

    def core_copy(c, h):
        return remote(
            core_out.at[c, h], core_in.at[c, h], core_send.at[c, h], core_recv.at[c, h], partner
        )

    def ring_copy(c, kind):
        return remote(
            ring_out.at[c, kind], ring_in.at[c, kind], ring_send.at[c, kind],
            ring_recv.at[c, kind], right if kind % 2 == 0 else left,
        )

    def multiply(c):
        for h in range(2):
            if c == 0:
                hidden_loads[h].wait()
            product = lax.dot_general(
                weights[c], hidden[h * HALF : (h + 1) * HALF],
                (((1,), (1,)), ((), ())), preferred_element_type=F32,
            )
            core_out[c, h] = product[:128].astype(BF16)
            own[c, h] = product[128:]

    def core_go(c):
        for h in range(2):
            core_copy(c, h).start()

    def combine(c):
        def summed(h, row):
            return own[c, h, row : row + 32] + core_in[c, h, row : row + 32].astype(F32)

        for h in range(2):
            core_copy(c, h).wait_recv()
            ring_out[c, h] = summed(h, 64).astype(BF16)
            ring_copy(c, h).start()
        for h in range(2):
            kind = 3 if h == 0 else 2
            ring_out[c, kind] = summed(h, 96 if h == 0 else 32).astype(BF16)
            ring_copy(c, kind).start()
        for h in range(2):
            for row in (32 if h == 0 else 96, 0):
                own[c, h, row : row + 32] = summed(h, row)

    def pass_on(c):
        for h in range(2):
            ring_copy(c, h).wait_recv()
            later = 32 if h == 0 else 96
            ring_out[c, 4 + h] = (
                own[c, h, later : later + 32] + ring_in[c, h].astype(F32)
            ).astype(BF16)
            ring_copy(c, 4 + h).start()

    def finish(c):
        for h in range(2):
            kinds = (3, 4) if h == 0 else (2, 5)
            total = own[c, h, 0:32]
            for kind in kinds:
                ring_copy(c, kind).wait_recv()
                total = total + ring_in[c, kind].astype(F32)
            if c >= MIXES:
                gates[pl.ds((c - MIXES) * 32, 32), pl.ds(h * HALF, HALF)] = total
            else:
                spread(total[:16] * total[16:], h)
        if c < MIXES:
            for peer in range(16):
                mixed_out[c, peer * 16 : peer * 16 + 16] = relay[pl.ds(peer, 16, stride=16), :].astype(BF16)
            exchange(
                rows_of(mixed_out.at[c]), rows_of(mixed_in.at[c]), mixed_send.at[c],
                mixed_recv.at[c],
            )

    def transformed(signals):
        wide = jnp.concatenate(signals, axis=1)
        value = dot(first[0], wide) + dot(first[1], wide)
        parts = []
        for n in range(len(signals)):
            real = value[:ROWS, n * COLS : (n + 1) * COLS]
            imag = value[ROWS:, n * COLS : (n + 1) * COLS]
            parts.append(
                jnp.concatenate(
                    [real * turn[0] - imag * turn[1], real * turn[1] + imag * turn[0]], axis=1
                )
            )
        high, low = halves_of(jnp.concatenate(parts, axis=0))
        return dot(high, ahead[0]) + dot(high, ahead[1]) + dot(low, ahead[0])

    def arrange_taps():
        taps_load.wait()
        for q in range(MIXES):
            for h in range(2):
                spread(taps[q * 16 : q * 16 + 16, h * HALF : (h + 1) * HALF].astype(F32), h)
            for peer in range(16):
                taps_out[peer, q] = relay[pl.ds(peer, 16, stride=16), :].astype(BF16)

    def send_taps():
        exchange(lambda peer: taps_out.at[peer], lambda peer: taps_in.at[peer], taps_send, taps_recv)

    def filter_spectra():
        exchange_arrived(taps_out, taps_in, taps_recv)
        for copy in table_loads:
            copy.wait()
        value = transformed([taps_in[:, q].reshape(ROWS, COLS) for q in range(MIXES)])
        spectrum[...] = value.reshape(MIXES, ROWS, 2 * COLS)

    def convolve(q):
        exchange_arrived(mixed_out.at[q], mixed_in.at[q], mixed_recv.at[q])
        value = transformed([mixed_in[q]])
        real, imag = value[:, :COLS], value[:, COLS:]
        freal, fimag = spectrum[q, :, :COLS], spectrum[q, :, COLS:]
        value = jnp.concatenate(
            [real * freal - imag * fimag, real * fimag + imag * freal], axis=1
        )
        high, low = halves_of(value)
        value = dot(high, back[0]) + dot(high, back[1]) + dot(low, back[0])
        real, imag = value[:, :COLS], value[:, COLS:]
        value = jnp.concatenate(
            [real * turn[0] + imag * turn[1], imag * turn[0] - real * turn[1]], axis=0
        )
        high, low = halves_of(value)
        conv_out[q] = dot(last[0], high) + dot(last[0], low) + dot(last[1], high)
        exchange(rows_of(conv_out.at[q]), rows_of(conv_in.at[q]), conv_send.at[q], conv_recv.at[q])

    def emit(q):
        exchange_arrived(conv_out.at[q], conv_in.at[q], conv_recv.at[q])
        rows = pl.ds(q * 16, 16)
        for tile in range(16):
            lanes = pl.ds(tile * COLS, COLS)
            part = conv_in[q, pl.ds(tile, 16, stride=16), :]
            gated[rows, lanes] = (gates[rows, lanes] * part).astype(BF16)
        pltpu.make_async_copy(gated.at[rows], out_hbm.at[rows], store_sem.at[q]).start()

    turn_weights(1)
    turn_weights(2)
    multiply(0)
    multiply(1)
    pl.semaphore_wait(barrier, 7)
    for near in around:
        signal(near_sem, near)
    core_go(0)
    core_go(1)
    multiply(2)
    core_go(2)
    arrange_taps()
    combine(0)
    combine(1)
    pl.semaphore_wait(near_sem, 4)
    for far in across:
        signal(far_sem, far)
    turn_weights(0)
    pass_on(0)
    multiply(3)
    core_go(3)
    pl.semaphore_wait(far_sem, 2)
    send_taps()
    combine(2)
    pass_on(1)
    finish(0)
    multiply(4)
    core_go(4)
    filter_spectra()
    combine(3)
    pass_on(2)
    finish(1)
    convolve(0)
    pass_on(3)
    combine(4)
    finish(2)
    multiply(5)
    core_go(5)
    convolve(1)
    combine(5)
    pass_on(4)
    finish(3)
    convolve(2)
    pass_on(5)
    convolve(3)
    finish(4)
    emit(0)
    emit(1)
    finish(5)
    emit(2)
    emit(3)

    for c in range(CHUNKS):
        for h in range(2):
            core_copy(c, h).wait_send()
        for kind in range(6):
            ring_copy(c, kind).wait_send()
    exchange_left(taps_out, taps_in, taps_send, blocks - 1)
    for q in range(MIXES):
        exchange_left(mixed_out.at[q], mixed_in.at[q], mixed_send.at[q], (blocks - 1) * 16)
        exchange_left(conv_out.at[q], conv_in.at[q], conv_send.at[q], (blocks - 1) * 16)
        rows = pl.ds(q * 16, 16)
        pltpu.make_async_copy(gated.at[rows], out_hbm.at[rows], store_sem.at[q]).wait()


def per_device(hidden_in, projection, filter_taps):
    tables = transform_tables()
    blocks = lax.axis_size("seq")
    anywhere = pl.BlockSpec(memory_space=pl.ANY)
    dma = pltpu.SemaphoreType.DMA
    return pl.pallas_call(
        kernel,
        out_shape=jax.ShapeDtypeStruct(filter_taps.shape, BF16),
        in_specs=[anywhere] * (3 + len(tables)),
        out_specs=anywhere,
        scratch_shapes=[
            pltpu.VMEM(hidden_in.shape, BF16),
            pltpu.VMEM(projection.shape, BF16),
            pltpu.VMEM(filter_taps.shape, BF16),
        ]
        + [pltpu.VMEM(table.shape, table.dtype) for table in tables]
        + [
            pltpu.VMEM((CHUNKS, 256, hidden_in.shape[1]), BF16),
            pltpu.VMEM((CHUNKS, 2, 128, HALF), F32),
            pltpu.VMEM((CHUNKS, 2, 128, HALF), BF16),
            pltpu.VMEM((CHUNKS, 2, 128, HALF), BF16),
            pltpu.VMEM((CHUNKS, 6, 32, HALF), BF16),
            pltpu.VMEM((CHUNKS, 6, 32, HALF), BF16),
            pltpu.VMEM((256, COLS), F32),
            pltpu.VMEM((blocks, MIXES, 16, COLS), BF16),
            pltpu.VMEM((blocks, MIXES, 16, COLS), BF16),
            pltpu.VMEM((MIXES, ROWS, COLS), BF16),
            pltpu.VMEM((MIXES, ROWS, COLS), BF16),
            pltpu.VMEM((MIXES, ROWS, 2 * COLS), F32),
            pltpu.VMEM((MIXES, ROWS, COLS), F32),
            pltpu.VMEM((MIXES, ROWS, COLS), F32),
            pltpu.VMEM(filter_taps.shape, F32),
            pltpu.VMEM(filter_taps.shape, BF16),
            dma((11,)),
            dma((CHUNKS, 2)),
            dma((CHUNKS, 2)),
            dma((CHUNKS, 6)),
            dma((CHUNKS, 6)),
            dma(()),
            dma(()),
            dma((MIXES,)),
            dma((MIXES,)),
            dma((MIXES,)),
            dma((MIXES,)),
            dma((MIXES,)),
            pltpu.SemaphoreType.REGULAR,
            pltpu.SemaphoreType.REGULAR,
        ],
        compiler_params=pltpu.CompilerParams(
            collective_id=0, has_side_effects=True, vmem_limit_bytes=60 * 1024 * 1024
        ),
        cost_estimate=pl.CostEstimate(
            flops=7_000_000_000, bytes_accessed=8_000_000, transcendentals=0
        ),
    )(hidden_in, projection, filter_taps, *[jnp.asarray(table) for table in tables])


def solution(mesh):
    placed = (P("seq", "chan"), P(None, "chan", None), P("chan", "seq"))
    return jax.shard_map(
        per_device, mesh=mesh, in_specs=placed, out_specs=P("chan", "seq"), check_vma=False
    )
```

```python
import functools

import jax
import jax.numpy as jnp
import numpy as np
from jax import lax
from jax.experimental import pallas as pl
from jax.experimental.pallas import tpu as pltpu
from jax.sharding import PartitionSpec as P

ROWS, COLS = 256, 128
CHUNKS = 6
MIXES = 4
HALF = 1024
TILE = 256
BF16 = jnp.bfloat16
F32 = jnp.float32


def split_table(table):
    high = np.asarray(table, np.float32).astype(BF16)
    low = (np.asarray(table, np.float64) - high.astype(np.float64)).astype(np.float32).astype(BF16)
    return np.stack([high, low])


def transform_tables():
    total = ROWS * COLS
    counter = np.arange(ROWS)
    outer = 2.0 * np.pi * ((counter[:, None] * (4 * counter[None, :] + 1)) % (4 * ROWS)) / (4 * ROWS)
    inner = np.arange(COLS)
    twist = 2.0 * np.pi * (inner[None, :] * (4 * counter[:, None] + 1)) / (4 * total)
    second = 2.0 * np.pi * ((inner[:, None] * inner[None, :]) % COLS) / COLS
    first = np.concatenate([np.cos(outer.T), -np.sin(outer.T)], axis=0)
    last = np.concatenate([np.cos(outer), -np.sin(outer)], axis=1) / total
    cos2, sin2 = np.cos(second), np.sin(second)
    ahead = np.block([[cos2, -sin2], [sin2, cos2]])
    back = np.block([[cos2, sin2], [-sin2, cos2]])
    turn = np.stack([np.cos(twist), -np.sin(twist)]).astype(np.float32)
    return (
        split_table(first),
        split_table(ahead),
        split_table(back),
        split_table(last),
        turn,
    )


def dot(left, right):
    return jnp.dot(left, right, preferred_element_type=F32)


def halves_of(value):
    high = value.astype(BF16)
    return high, (value - high.astype(F32)).astype(BF16)


def kernel(
    hidden_hbm, proj_hbm, taps_hbm, first_hbm, ahead_hbm, back_hbm, last_hbm, turn_hbm,
    out_hbm,
    hidden, proj, taps, first, ahead, back, last, turn,
    weights, own, core_out, core_in, ring_out, ring_in,
    relay, taps_out, taps_in, mixed_out, mixed_in, spectrum, conv_out, conv_in, gates, gated,
    load_sem, core_send, core_recv, ring_send, ring_recv,
    taps_send, taps_recv, mixed_send, mixed_recv, conv_send, conv_recv, store_sem, walk_sem,
):
    seq = lax.axis_index("seq")
    chan = lax.axis_index("chan")
    blocks = lax.axis_size("seq")
    y = chan // 2
    core = lax.rem(chan, 2)
    partner = {"chan": y * 2 + 1 - core}
    right = {"chan": lax.rem(y + 1, 4) * 2 + core}
    left = {"chan": lax.rem(y + 3, 4) * 2 + core}

    def signal(semaphore, device):
        pl.semaphore_signal(
            semaphore, inc=1, device_id=device, device_id_type=pl.DeviceIdType.MESH
        )

    side = 4
    z, x = seq // side, lax.rem(seq, side)
    odd = lax.rem(z, 2)
    place = z * side + x + odd * (side - 1 - 2 * x)

    def walk(by):
        spot = lax.rem(place + by + blocks, blocks)
        row, col = spot // side, lax.rem(spot, side)
        flipped = lax.rem(row, 2)
        return {"seq": row * side + col + flipped * (side - 1 - 2 * col)}

    loads = []

    def load(src, dst):
        copy = pltpu.make_async_copy(src, dst, load_sem.at[len(loads)])
        copy.start()
        loads.append(copy)
        return copy

    proj_loads = [None, load(proj_hbm.at[1], proj.at[1]), load(proj_hbm.at[2], proj.at[2])]
    hidden_loads = [
        load(hidden_hbm.at[pl.ds(n * HALF, HALF)], hidden.at[pl.ds(n * HALF, HALF)])
        for n in range(2)
    ]
    barrier = pltpu.get_barrier_semaphore()
    for device in (right, left, walk(1), partner):
        signal(barrier, device)
    taps_load = load(taps_hbm, taps)
    proj_loads[0] = load(proj_hbm.at[0], proj.at[0])
    table_loads = [
        load(first_hbm, first),
        load(ahead_hbm, ahead),
        load(back_hbm, back),
        load(last_hbm, last),
        load(turn_hbm, turn),
    ]

    rounds = ((-1,), (-1, 1), (-2, 2), (-4, 4))

    def tell(n):
        for by in rounds[n]:
            signal(walk_sem.at[n], walk(by))

    def hear(n):
        pl.semaphore_wait(walk_sem.at[n], len(rounds[n]))

    def remote(src, dst, send, recv, device):
        return pltpu.make_async_remote_copy(
            src_ref=src, dst_ref=dst, send_sem=send, recv_sem=recv,
            device_id=device, device_id_type=pl.DeviceIdType.MESH,
        )

    def exchange(src, dst, send, recv):
        pltpu.make_async_copy(src(seq), dst(seq), recv).start()

        def send_to(step):
            peer = lax.rem(z + step // side, side) * side + lax.rem(x + step, side)
            remote(src(peer), dst(seq), send, recv, {"seq": peer}).start()

        pl.loop(10, blocks)(send_to)
        pl.loop(1, 10)(lambda step: send_to(10 - step))

    def exchange_arrived(src, dst, recv):
        pltpu.make_async_copy(src, dst, recv).wait()

    def exchange_left(src, dst, send, count):
        pltpu.make_async_copy(src.at[pl.ds(0, count)], dst.at[pl.ds(0, count)], send).wait()

    def rows_of(ref):
        return lambda peer: ref.at[pl.ds(pl.multiple_of(peer * 16, 16), 16)]

    def spread(block, part):
        for tile in range(HALF // COLS):
            relay[pl.ds((part * (HALF // COLS) + tile) * 16, 16), :] = block[
                :, tile * COLS : (tile + 1) * COLS
            ]

    def turn_weights(kind):
        proj_loads[kind].wait()
        for ahead_by in range(4):
            lane = pl.multiple_of(lax.rem(y + ahead_by, 4) * 128, 128)
            turned = proj[kind, :, pl.ds(lane, 128)].T
            for side in range(2):
                place = (1 - core if side == 0 else core) * 128 + 32 * ahead_by
                if kind == 0:
                    for part in range(2):
                        row = pl.multiple_of(place, 32)
                        weights[MIXES + part, pl.ds(row, 32), :] = turned[
                            side * 64 + 32 * part : side * 64 + 32 * part + 32
                        ]
                else:
                    for part in range(MIXES):
                        row = pl.multiple_of(place + 16 * (kind - 1), 16)
                        weights[part, pl.ds(row, 16), :] = turned[
                            side * 64 + 16 * part : side * 64 + 16 * part + 16
                        ]

    pieces = ((2, 0), (2, 1), (1, 1), (3, 0), (1, 0), (3, 1), (0, 0), (0, 1))
    groups = ((0, 2), (2, 2), (4, 4))

    def core_copy(c, group):
        part = pl.ds(*groups[group])
        return remote(
            core_out.at[c, part], core_in.at[c, part], core_send.at[c, group],
            core_recv.at[c, group], partner,
        )

    def summed(c, piece):
        return own[c, piece] + core_in[c, piece].astype(F32)

    def ring_copy(c, kind):
        return remote(
            ring_out.at[c, kind], ring_in.at[c, kind], ring_send.at[c, kind],
            ring_recv.at[c, kind], right if kind % 2 == 0 else left,
        )

    def multiply(c):
        for h in range(2):
            if c == 0:
                hidden_loads[h].wait()
            product = lax.dot_general(
                weights[c], hidden[h * HALF : (h + 1) * HALF],
                (((1,), (1,)), ((), ())), preferred_element_type=F32,
            )
            for piece, (owner, half) in enumerate(pieces):
                if half == h:
                    core_out[c, piece] = product[owner * 32 : owner * 32 + 32].astype(BF16)
                    own[c, piece] = product[128 + owner * 32 : 160 + owner * 32]

    def core_go(c):
        for group in range(3):
            core_copy(c, group).start()

    def send_pieces(c, group):
        core_copy(c, group).wait_recv()
        for kind in (2 * group, 2 * group + 1):
            ring_out[c, kind] = summed(c, kind).astype(BF16)
            ring_copy(c, kind).start()

    def far(c):
        send_pieces(c, 0)

    def near(c):
        send_pieces(c, 1)

    def pass_on(c):
        core_copy(c, 2).wait_recv()
        for h in range(2):
            ring_copy(c, h).wait_recv()
            ring_out[c, 4 + h] = (summed(c, 4 + h) + ring_in[c, h].astype(F32)).astype(BF16)
            ring_copy(c, 4 + h).start()

    def finish(c):
        for h in range(2):
            total = summed(c, 6 + h)
            for kind in (3, 4) if h == 0 else (2, 5):
                ring_copy(c, kind).wait_recv()
                total = total + ring_in[c, kind].astype(F32)
            if c >= MIXES:
                gates[pl.ds((c - MIXES) * 32, 32), pl.ds(h * HALF, HALF)] = total
            else:
                spread(total[:16] * total[16:], h)
        if c < MIXES:
            for peer in range(16):
                mixed_out[c, peer * 16 : peer * 16 + 16] = relay[
                    pl.ds(peer, 16, stride=16), :
                ].astype(BF16)
            exchange(
                rows_of(mixed_out.at[c]), rows_of(mixed_in.at[c]), mixed_send.at[c],
                mixed_recv.at[c],
            )

    def transformed(signals):
        wide = jnp.concatenate(signals, axis=1)
        value = dot(first[0], wide) + dot(first[1], wide)
        parts = []
        for n in range(len(signals)):
            real = value[:ROWS, n * COLS : (n + 1) * COLS]
            imag = value[ROWS:, n * COLS : (n + 1) * COLS]
            parts.append(
                jnp.concatenate(
                    [real * turn[0] - imag * turn[1], real * turn[1] + imag * turn[0]], axis=1
                )
            )
        high, low = halves_of(jnp.concatenate(parts, axis=0))
        return dot(high, ahead[0]) + dot(high, ahead[1]) + dot(low, ahead[0])

    def arrange_taps():
        taps_load.wait()
        for q in range(MIXES):
            for h in range(2):
                spread(taps[q * 16 : q * 16 + 16, h * HALF : (h + 1) * HALF].astype(F32), h)
            for peer in range(16):
                taps_out[peer, q] = relay[pl.ds(peer, 16, stride=16), :].astype(BF16)

    def send_taps():
        exchange(lambda peer: taps_out.at[peer], lambda peer: taps_in.at[peer], taps_send, taps_recv)

    def filter_spectra():
        exchange_arrived(taps_out, taps_in, taps_recv)
        for copy in table_loads:
            copy.wait()
        value = transformed([taps_in[:, q].reshape(ROWS, COLS) for q in range(MIXES)])
        spectrum[...] = value.reshape(MIXES, ROWS, 2 * COLS)

    def convolve(q):
        exchange_arrived(mixed_out.at[q], mixed_in.at[q], mixed_recv.at[q])
        value = transformed([mixed_in[q]])
        real, imag = value[:, :COLS], value[:, COLS:]
        freal, fimag = spectrum[q, :, :COLS], spectrum[q, :, COLS:]
        value = jnp.concatenate(
            [real * freal - imag * fimag, real * fimag + imag * freal], axis=1
        )
        high, low = halves_of(value)
        value = dot(high, back[0]) + dot(high, back[1]) + dot(low, back[0])
        real, imag = value[:, :COLS], value[:, COLS:]
        value = jnp.concatenate(
            [real * turn[0] + imag * turn[1], imag * turn[0] - real * turn[1]], axis=0
        )
        high, low = halves_of(value)
        conv_out[q] = dot(last[0], high) + dot(last[0], low) + dot(last[1], high)
        exchange(rows_of(conv_out.at[q]), rows_of(conv_in.at[q]), conv_send.at[q], conv_recv.at[q])

    def emit(q):
        exchange_arrived(conv_out.at[q], conv_in.at[q], conv_recv.at[q])
        rows = pl.ds(q * 16, 16)
        for tile in range(16):
            lanes = pl.ds(tile * COLS, COLS)
            part = conv_in[q, pl.ds(tile, 16, stride=16), :]
            gated[rows, lanes] = (gates[rows, lanes] * part).astype(BF16)
        pltpu.make_async_copy(gated.at[rows], out_hbm.at[rows], store_sem.at[q]).start()

    turn_weights(1)
    turn_weights(2)
    multiply(0)
    pl.semaphore_wait(barrier, 4)
    core_go(0)
    tell(0)
    multiply(1)
    core_go(1)
    far(0)
    near(0)
    hear(0)
    tell(1)
    multiply(2)
    core_go(2)
    far(1)
    hear(1)
    tell(2)
    arrange_taps()
    turn_weights(0)
    multiply(3)
    core_go(3)
    pass_on(0)
    near(1)
    far(2)
    hear(2)
    tell(3)
    multiply(4)
    core_go(4)
    hear(3)
    send_taps()
    pass_on(1)
    near(2)
    far(3)
    multiply(5)
    core_go(5)
    finish(0)
    pass_on(2)
    near(3)
    filter_spectra()
    finish(1)
    pass_on(3)
    far(4)
    near(4)
    convolve(0)
    finish(2)
    far(5)
    finish(3)
    convolve(1)
    pass_on(4)
    near(5)
    convolve(2)
    pass_on(5)
    convolve(3)
    finish(4)
    emit(0)
    emit(1)
    finish(5)
    emit(2)
    emit(3)

    for c in range(CHUNKS):
        for group in range(3):
            core_copy(c, group).wait_send()
        for kind in range(6):
            ring_copy(c, kind).wait_send()
    exchange_left(taps_out, taps_in, taps_send, blocks - 1)
    for q in range(MIXES):
        exchange_left(mixed_out.at[q], mixed_in.at[q], mixed_send.at[q], (blocks - 1) * 16)
        exchange_left(conv_out.at[q], conv_in.at[q], conv_send.at[q], (blocks - 1) * 16)
        rows = pl.ds(q * 16, 16)
        pltpu.make_async_copy(gated.at[rows], out_hbm.at[rows], store_sem.at[q]).wait()


def per_device(hidden_in, projection, filter_taps):
    tables = transform_tables()
    blocks = lax.axis_size("seq")
    anywhere = pl.BlockSpec(memory_space=pl.ANY)
    dma = pltpu.SemaphoreType.DMA
    return pl.pallas_call(
        kernel,
        out_shape=jax.ShapeDtypeStruct(filter_taps.shape, BF16),
        in_specs=[anywhere] * (3 + len(tables)),
        out_specs=anywhere,
        scratch_shapes=[
            pltpu.VMEM(hidden_in.shape, BF16),
            pltpu.VMEM(projection.shape, BF16),
            pltpu.VMEM(filter_taps.shape, BF16),
        ]
        + [pltpu.VMEM(table.shape, table.dtype) for table in tables]
        + [
            pltpu.VMEM((CHUNKS, 256, hidden_in.shape[1]), BF16),
            pltpu.VMEM((CHUNKS, 8, 32, HALF), F32),
            pltpu.VMEM((CHUNKS, 8, 32, HALF), BF16),
            pltpu.VMEM((CHUNKS, 8, 32, HALF), BF16),
            pltpu.VMEM((CHUNKS, 6, 32, HALF), BF16),
            pltpu.VMEM((CHUNKS, 6, 32, HALF), BF16),
            pltpu.VMEM((256, COLS), F32),
            pltpu.VMEM((blocks, MIXES, 16, COLS), BF16),
            pltpu.VMEM((blocks, MIXES, 16, COLS), BF16),
            pltpu.VMEM((MIXES, ROWS, COLS), BF16),
            pltpu.VMEM((MIXES, ROWS, COLS), BF16),
            pltpu.VMEM((MIXES, ROWS, 2 * COLS), F32),
            pltpu.VMEM((MIXES, ROWS, COLS), F32),
            pltpu.VMEM((MIXES, ROWS, COLS), F32),
            pltpu.VMEM(filter_taps.shape, F32),
            pltpu.VMEM(filter_taps.shape, BF16),
            dma((11,)),
            dma((CHUNKS, 3)),
            dma((CHUNKS, 3)),
            dma((CHUNKS, 6)),
            dma((CHUNKS, 6)),
            dma(()),
            dma(()),
            dma((MIXES,)),
            dma((MIXES,)),
            dma((MIXES,)),
            dma((MIXES,)),
            dma((MIXES,)),
            pltpu.SemaphoreType.REGULAR((4,)),
        ],
        compiler_params=pltpu.CompilerParams(
            collective_id=0, has_side_effects=True, vmem_limit_bytes=60 * 1024 * 1024
        ),
        cost_estimate=pl.CostEstimate(
            flops=7_000_000_000, bytes_accessed=8_000_000, transcendentals=0
        ),
    )(hidden_in, projection, filter_taps, *[jnp.asarray(table) for table in tables])


def solution(mesh):
    placed = (P("seq", "chan"), P(None, "chan", None), P("chan", "seq"))
    return jax.shard_map(
        per_device, mesh=mesh, in_specs=placed, out_specs=P("chan", "seq"), check_vma=False
    )
```

```python
import functools

import jax
import jax.numpy as jnp
import numpy as np
from jax import lax
from jax.experimental import pallas as pl
from jax.experimental.pallas import tpu as pltpu
from jax.sharding import PartitionSpec as P

ROWS, COLS = 256, 128
CHUNKS = 6
MIXES = 4
HALF = 1024
TILE = 256
BF16 = jnp.bfloat16
F32 = jnp.float32


def split_table(table):
    high = np.asarray(table, np.float32).astype(BF16)
    low = (np.asarray(table, np.float64) - high.astype(np.float64)).astype(np.float32).astype(BF16)
    return np.stack([high, low])


def transform_tables():
    total = ROWS * COLS
    counter = np.arange(ROWS)
    outer = 2.0 * np.pi * ((counter[:, None] * (4 * counter[None, :] + 1)) % (4 * ROWS)) / (4 * ROWS)
    inner = np.arange(COLS)
    twist = 2.0 * np.pi * (inner[None, :] * (4 * counter[:, None] + 1)) / (4 * total)
    second = 2.0 * np.pi * ((inner[:, None] * inner[None, :]) % COLS) / COLS
    first = np.concatenate([np.cos(outer.T), -np.sin(outer.T)], axis=0)
    last = np.concatenate([np.cos(outer), -np.sin(outer)], axis=1) / total
    cos2, sin2 = np.cos(second), np.sin(second)
    ahead = np.block([[cos2, -sin2], [sin2, cos2]])
    back = np.block([[cos2, sin2], [-sin2, cos2]])
    turn = np.stack([np.cos(twist), -np.sin(twist)]).astype(np.float32)
    return (
        split_table(first),
        split_table(ahead),
        split_table(back),
        split_table(last),
        turn,
    )


def dot(left, right):
    return jnp.dot(left, right, preferred_element_type=F32)


def halves_of(value):
    high = value.astype(BF16)
    return high, (value - high.astype(F32)).astype(BF16)


def kernel(
    hidden_hbm, proj_hbm, taps_hbm, first_hbm, ahead_hbm, back_hbm, last_hbm, turn_hbm,
    out_hbm,
    hidden, proj, taps, first, ahead, back, last, turn,
    weights, own, core_out, core_in, ring_out, ring_in,
    relay, taps_out, taps_in, mixed_out, mixed_in, spectrum, conv_out, conv_in, gates, gated,
    load_sem, core_send, core_recv, ring_send, ring_recv,
    taps_send, taps_recv, mixed_send, mixed_recv, conv_send, conv_recv, store_sem, walk_sem,
):
    seq = lax.axis_index("seq")
    chan = lax.axis_index("chan")
    blocks = lax.axis_size("seq")
    y = chan // 2
    core = lax.rem(chan, 2)
    partner = {"chan": y * 2 + 1 - core}
    right = {"chan": lax.rem(y + 1, 4) * 2 + core}
    left = {"chan": lax.rem(y + 3, 4) * 2 + core}

    def signal(semaphore, device):
        pl.semaphore_signal(
            semaphore, inc=1, device_id=device, device_id_type=pl.DeviceIdType.MESH
        )

    side = 4
    z, x = seq // side, lax.rem(seq, side)
    odd = lax.rem(z, 2)
    place = z * side + x + odd * (side - 1 - 2 * x)

    def walk(by):
        spot = lax.rem(place + by + blocks, blocks)
        row, col = spot // side, lax.rem(spot, side)
        flipped = lax.rem(row, 2)
        return {"seq": row * side + col + flipped * (side - 1 - 2 * col)}

    loads = []

    def load(src, dst, now=True):
        copy = pltpu.make_async_copy(src, dst, load_sem.at[len(loads)])
        if now:
            copy.start()
        loads.append(copy)
        return copy

    proj_loads = [None, load(proj_hbm.at[1], proj.at[1]), load(proj_hbm.at[2], proj.at[2])]
    hidden_loads = [
        load(hidden_hbm.at[pl.ds(n * HALF, HALF)], hidden.at[pl.ds(n * HALF, HALF)])
        for n in range(2)
    ]
    barrier = pltpu.get_barrier_semaphore()
    for device in (right, left, walk(1), partner):
        signal(barrier, device)
    taps_load = load(taps_hbm, taps, False)
    proj_loads[0] = load(proj_hbm.at[0], proj.at[0], False)
    table_loads = [
        load(first_hbm, first, False),
        load(ahead_hbm, ahead, False),
        load(back_hbm, back, False),
        load(last_hbm, last, False),
        load(turn_hbm, turn, False),
    ]

    def load_rest():
        for copy in loads[4:]:
            copy.start()

    rounds = ((-1,), (-1, 1), (-2, 2), (-4, 4))

    def tell(n):
        for by in rounds[n]:
            signal(walk_sem.at[n], walk(by))

    def hear(n):
        pl.semaphore_wait(walk_sem.at[n], len(rounds[n]))

    def remote(src, dst, send, recv, device):
        return pltpu.make_async_remote_copy(
            src_ref=src, dst_ref=dst, send_sem=send, recv_sem=recv,
            device_id=device, device_id_type=pl.DeviceIdType.MESH,
        )

    def hops(step):
        return sum(min(by, side - by) for by in divmod(step, side))

    peers = [
        lax.rem(z + step // side, side) * side + lax.rem(x + step % side, side)
        for step in sorted(range(1, side * side), key=hops, reverse=True)
    ]

    def exchange(src, dst, send, recv):
        pltpu.make_async_copy(src(seq), dst(seq), recv).start()

        for peer in peers:
            remote(src(peer), dst(seq), send, recv, {"seq": peer}).start()

    def exchange_arrived(src, dst, recv):
        pltpu.make_async_copy(src, dst, recv).wait()

    def exchange_left(src, dst, send, count):
        pltpu.make_async_copy(src.at[pl.ds(0, count)], dst.at[pl.ds(0, count)], send).wait()

    def rows_of(ref):
        return lambda peer: ref.at[pl.ds(pl.multiple_of(peer * 16, 16), 16)]

    def spread(block, part):
        for tile in range(HALF // COLS):
            relay[pl.ds((part * (HALF // COLS) + tile) * 16, 16), :] = block[
                :, tile * COLS : (tile + 1) * COLS
            ]

    def turn_weights(kind):
        proj_loads[kind].wait()
        for ahead_by in range(4):
            lane = pl.multiple_of(lax.rem(y + ahead_by, 4) * 128, 128)
            turned = proj[kind, :, pl.ds(lane, 128)].T
            for side in range(2):
                place = (1 - core if side == 0 else core) * 128 + 32 * ahead_by
                if kind == 0:
                    for part in range(2):
                        row = pl.multiple_of(place, 32)
                        weights[MIXES + part, pl.ds(row, 32), :] = turned[
                            side * 64 + 32 * part : side * 64 + 32 * part + 32
                        ]
                else:
                    for part in range(MIXES):
                        row = pl.multiple_of(place + 16 * (kind - 1), 16)
                        weights[part, pl.ds(row, 16), :] = turned[
                            side * 64 + 16 * part : side * 64 + 16 * part + 16
                        ]

    pieces = ((2, 0), (2, 1), (1, 1), (3, 0), (1, 0), (3, 1), (0, 0), (0, 1))
    def groups(c):
        return ((0, 2), (2, 2), (4, 4)) if c == 0 else ((0, 8),)

    def core_copy(c, group):
        part = pl.ds(*groups(c)[group])
        return remote(
            core_out.at[c, part], core_in.at[c, part], core_send.at[c, group],
            core_recv.at[c, group], partner,
        )

    def summed(c, piece):
        return own[c, piece] + core_in[c, piece].astype(F32)

    def ring_copy(c, kind):
        return remote(
            ring_out.at[c, kind], ring_in.at[c, kind], ring_send.at[c, kind],
            ring_recv.at[c, kind], right if kind % 2 == 0 else left,
        )

    def multiply(c):
        for h in range(2):
            if c == 0:
                hidden_loads[h].wait()
            product = lax.dot_general(
                weights[c], hidden[h * HALF : (h + 1) * HALF],
                (((1,), (1,)), ((), ())), preferred_element_type=F32,
            )
            for piece, (owner, half) in enumerate(pieces):
                if half == h:
                    core_out[c, piece] = product[owner * 32 : owner * 32 + 32].astype(BF16)
                    own[c, piece] = product[128 + owner * 32 : 160 + owner * 32]

    def core_go(c):
        for group in range(len(groups(c))):
            core_copy(c, group).start()

    def send_pieces(c, group):
        if group < len(groups(c)):
            core_copy(c, group).wait_recv()
        for kind in (2 * group, 2 * group + 1):
            ring_out[c, kind] = summed(c, kind).astype(BF16)
            ring_copy(c, kind).start()

    def far(c):
        send_pieces(c, 0)

    def near(c):
        send_pieces(c, 1)

    def pass_on(c):
        if c == 0:
            core_copy(c, 2).wait_recv()
        for h in range(2):
            ring_copy(c, h).wait_recv()
            ring_out[c, 4 + h] = (summed(c, 4 + h) + ring_in[c, h].astype(F32)).astype(BF16)
            ring_copy(c, 4 + h).start()

    def finish(c):
        for h in range(2):
            total = summed(c, 6 + h)
            for kind in (3, 4) if h == 0 else (2, 5):
                ring_copy(c, kind).wait_recv()
                total = total + ring_in[c, kind].astype(F32)
            if c >= MIXES:
                gates[pl.ds((c - MIXES) * 32, 32), pl.ds(h * HALF, HALF)] = total
            else:
                spread(total[:16] * total[16:], h)
        if c < MIXES:
            for peer in range(16):
                mixed_out[c, peer * 16 : peer * 16 + 16] = relay[
                    pl.ds(peer, 16, stride=16), :
                ].astype(BF16)
            exchange(
                rows_of(mixed_out.at[c]), rows_of(mixed_in.at[c]), mixed_send.at[c],
                mixed_recv.at[c],
            )

    def transformed(signals):
        wide = jnp.concatenate(signals, axis=1)
        value = dot(first[0], wide) + dot(first[1], wide)
        parts = []
        for n in range(len(signals)):
            real = value[:ROWS, n * COLS : (n + 1) * COLS]
            imag = value[ROWS:, n * COLS : (n + 1) * COLS]
            parts.append(
                jnp.concatenate(
                    [real * turn[0] - imag * turn[1], real * turn[1] + imag * turn[0]], axis=1
                )
            )
        high, low = halves_of(jnp.concatenate(parts, axis=0))
        return dot(high, ahead[0]) + dot(high, ahead[1]) + dot(low, ahead[0])

    def arrange_taps():
        taps_load.wait()
        for q in range(MIXES):
            for h in range(2):
                spread(taps[q * 16 : q * 16 + 16, h * HALF : (h + 1) * HALF].astype(F32), h)
            for peer in range(16):
                taps_out[peer, q] = relay[pl.ds(peer, 16, stride=16), :].astype(BF16)

    def send_taps():
        exchange(lambda peer: taps_out.at[peer], lambda peer: taps_in.at[peer], taps_send, taps_recv)

    def filter_spectra():
        exchange_arrived(taps_out, taps_in, taps_recv)
        for copy in table_loads:
            copy.wait()
        value = transformed([taps_in[:, q].reshape(ROWS, COLS) for q in range(MIXES)])
        spectrum[...] = value.reshape(MIXES, ROWS, 2 * COLS)

    def convolve(q):
        exchange_arrived(mixed_out.at[q], mixed_in.at[q], mixed_recv.at[q])
        value = transformed([mixed_in[q]])
        real, imag = value[:, :COLS], value[:, COLS:]
        freal, fimag = spectrum[q, :, :COLS], spectrum[q, :, COLS:]
        value = jnp.concatenate(
            [real * freal - imag * fimag, real * fimag + imag * freal], axis=1
        )
        high, low = halves_of(value)
        value = dot(high, back[0]) + dot(high, back[1]) + dot(low, back[0])
        real, imag = value[:, :COLS], value[:, COLS:]
        value = jnp.concatenate(
            [real * turn[0] + imag * turn[1], imag * turn[0] - real * turn[1]], axis=0
        )
        high, low = halves_of(value)
        value = dot(last[0], high) + dot(last[0], low) + dot(last[1], high)
        conv_out[q] = value.astype(BF16)
        exchange(rows_of(conv_out.at[q]), rows_of(conv_in.at[q]), conv_send.at[q], conv_recv.at[q])

    def emit(q):
        exchange_arrived(conv_out.at[q], conv_in.at[q], conv_recv.at[q])
        rows = pl.ds(q * 16, 16)
        relay[...] = conv_in[q].astype(F32)
        for tile in range(16):
            lanes = pl.ds(tile * COLS, COLS)
            part = relay[pl.ds(tile, 16, stride=16), :]
            gated[rows, lanes] = (gates[rows, lanes] * part).astype(BF16)
        pltpu.make_async_copy(gated.at[rows], out_hbm.at[rows], store_sem.at[q]).start()

    turn_weights(1)
    turn_weights(2)
    multiply(0)
    pl.semaphore_wait(barrier, 4)
    core_go(0)
    load_rest()
    tell(0)
    multiply(1)
    core_go(1)
    far(0)
    near(0)
    hear(0)
    tell(1)
    multiply(2)
    core_go(2)
    far(1)
    hear(1)
    tell(2)
    arrange_taps()
    turn_weights(0)
    multiply(3)
    core_go(3)
    pass_on(0)
    near(1)
    far(2)
    hear(2)
    tell(3)
    multiply(4)
    core_go(4)
    hear(3)
    send_taps()
    pass_on(1)
    near(2)
    far(3)
    multiply(5)
    core_go(5)
    finish(0)
    pass_on(2)
    near(3)
    filter_spectra()
    finish(1)
    pass_on(3)
    far(4)
    near(4)
    far(5)
    near(5)
    convolve(0)
    finish(2)
    finish(3)
    convolve(1)
    pass_on(4)
    convolve(2)
    pass_on(5)
    convolve(3)
    finish(4)
    emit(0)
    emit(1)
    finish(5)
    emit(2)
    emit(3)

    for c in range(CHUNKS):
        for group in range(len(groups(c))):
            core_copy(c, group).wait_send()
        for kind in range(6):
            ring_copy(c, kind).wait_send()
    exchange_left(taps_out, taps_in, taps_send, blocks - 1)
    for q in range(MIXES):
        exchange_left(mixed_out.at[q], mixed_in.at[q], mixed_send.at[q], (blocks - 1) * 16)
        exchange_left(conv_out.at[q], conv_in.at[q], conv_send.at[q], (blocks - 1) * 16)
        rows = pl.ds(q * 16, 16)
        pltpu.make_async_copy(gated.at[rows], out_hbm.at[rows], store_sem.at[q]).wait()


def per_device(hidden_in, projection, filter_taps):
    tables = transform_tables()
    blocks = lax.axis_size("seq")
    anywhere = pl.BlockSpec(memory_space=pl.ANY)
    dma = pltpu.SemaphoreType.DMA
    return pl.pallas_call(
        kernel,
        out_shape=jax.ShapeDtypeStruct(filter_taps.shape, BF16),
        in_specs=[anywhere] * (3 + len(tables)),
        out_specs=anywhere,
        scratch_shapes=[
            pltpu.VMEM(hidden_in.shape, BF16),
            pltpu.VMEM(projection.shape, BF16),
            pltpu.VMEM(filter_taps.shape, BF16),
        ]
        + [pltpu.VMEM(table.shape, table.dtype) for table in tables]
        + [
            pltpu.VMEM((CHUNKS, 256, hidden_in.shape[1]), BF16),
            pltpu.VMEM((CHUNKS, 8, 32, HALF), F32),
            pltpu.VMEM((CHUNKS, 8, 32, HALF), BF16),
            pltpu.VMEM((CHUNKS, 8, 32, HALF), BF16),
            pltpu.VMEM((CHUNKS, 6, 32, HALF), BF16),
            pltpu.VMEM((CHUNKS, 6, 32, HALF), BF16),
            pltpu.VMEM((256, COLS), F32),
            pltpu.VMEM((blocks, MIXES, 16, COLS), BF16),
            pltpu.VMEM((blocks, MIXES, 16, COLS), BF16),
            pltpu.VMEM((MIXES, ROWS, COLS), BF16),
            pltpu.VMEM((MIXES, ROWS, COLS), BF16),
            pltpu.VMEM((MIXES, ROWS, 2 * COLS), F32),
            pltpu.VMEM((MIXES, ROWS, COLS), BF16),
            pltpu.VMEM((MIXES, ROWS, COLS), BF16),
            pltpu.VMEM(filter_taps.shape, F32),
            pltpu.VMEM(filter_taps.shape, BF16),
            dma((11,)),
            dma((CHUNKS, 3)),
            dma((CHUNKS, 3)),
            dma((CHUNKS, 6)),
            dma((CHUNKS, 6)),
            dma(()),
            dma(()),
            dma((MIXES,)),
            dma((MIXES,)),
            dma((MIXES,)),
            dma((MIXES,)),
            dma((MIXES,)),
            pltpu.SemaphoreType.REGULAR((4,)),
        ],
        compiler_params=pltpu.CompilerParams(
            collective_id=0, has_side_effects=True, vmem_limit_bytes=60 * 1024 * 1024
        ),
        cost_estimate=pl.CostEstimate(
            flops=7_000_000_000, bytes_accessed=8_000_000, transcendentals=0
        ),
    )(hidden_in, projection, filter_taps, *[jnp.asarray(table) for table in tables])


def solution(mesh):
    placed = (P("seq", "chan"), P(None, "chan", None), P("chan", "seq"))
    return jax.shard_map(
        per_device, mesh=mesh, in_specs=placed, out_specs=P("chan", "seq"), check_vma=False
    )
```

```python
import functools

import jax
import jax.numpy as jnp
import numpy as np
from jax import lax
from jax.experimental import pallas as pl
from jax.experimental.pallas import tpu as pltpu
from jax.sharding import PartitionSpec as P

ROWS, COLS = 256, 128
CHUNKS = 6
MIXES = 4
HALF = 1024
TILE = 256
BF16 = jnp.bfloat16
F32 = jnp.float32


def split_table(table):
    high = np.asarray(table, np.float32).astype(BF16)
    low = (np.asarray(table, np.float64) - high.astype(np.float64)).astype(np.float32).astype(BF16)
    return np.stack([high, low])


def transform_tables():
    total = ROWS * COLS
    counter = np.arange(ROWS)
    outer = 2.0 * np.pi * ((counter[:, None] * (4 * counter[None, :] + 1)) % (4 * ROWS)) / (4 * ROWS)
    inner = np.arange(COLS)
    twist = 2.0 * np.pi * (inner[None, :] * (4 * counter[:, None] + 1)) / (4 * total)
    second = 2.0 * np.pi * ((inner[:, None] * inner[None, :]) % COLS) / COLS
    first = np.concatenate([np.cos(outer.T), -np.sin(outer.T)], axis=0)
    last = np.concatenate([np.cos(outer), -np.sin(outer)], axis=1) / total
    cos2, sin2 = np.cos(second), np.sin(second)
    ahead = np.block([[cos2, -sin2], [sin2, cos2]])
    back = np.block([[cos2, sin2], [-sin2, cos2]])
    turn = np.stack([np.cos(twist), -np.sin(twist)]).astype(np.float32)
    return (
        split_table(first),
        split_table(ahead),
        split_table(back),
        split_table(last),
        turn,
    )


def dot(left, right):
    return jnp.dot(left, right, preferred_element_type=F32)


def halves_of(value):
    high = value.astype(BF16)
    return high, (value - high.astype(F32)).astype(BF16)


def kernel(
    hidden_hbm, proj_hbm, taps_hbm, first_hbm, ahead_hbm, back_hbm, last_hbm, turn_hbm,
    out_hbm,
    hidden, proj, taps, first, ahead, back, last, turn,
    weights, own, core_out, core_in, ring_out, ring_in,
    relay, taps_out, taps_in, mixed_out, mixed_in, spectrum, conv_out, conv_in, gates, gated,
    load_sem, core_send, core_recv, ring_send, ring_recv,
    taps_send, taps_recv, mixed_send, mixed_recv, conv_send, conv_recv, store_sem,
):
    seq = lax.axis_index("seq")
    chan = lax.axis_index("chan")
    blocks = lax.axis_size("seq")
    y = chan // 2
    core = lax.rem(chan, 2)
    partner = {"chan": y * 2 + 1 - core}
    right = {"chan": lax.rem(y + 1, 4) * 2 + core}
    left = {"chan": lax.rem(y + 3, 4) * 2 + core}

    def signal(semaphore, device):
        pl.semaphore_signal(
            semaphore, inc=1, device_id=device, device_id_type=pl.DeviceIdType.MESH
        )

    side = 4
    z, x = seq // side, lax.rem(seq, side)

    loads = []

    def load(src, dst, now=True):
        copy = pltpu.make_async_copy(src, dst, load_sem.at[len(loads)])
        if now:
            copy.start()
        loads.append(copy)
        return copy

    proj_loads = [None, load(proj_hbm.at[1], proj.at[1]), load(proj_hbm.at[2], proj.at[2])]
    hidden_loads = [
        load(hidden_hbm.at[pl.ds(n * HALF, HALF)], hidden.at[pl.ds(n * HALF, HALF)])
        for n in range(2)
    ]
    barrier = pltpu.get_barrier_semaphore()
    for device in (right, left, partner):
        signal(barrier, device)
    for by in range(1, side * side):
        signal(barrier, {"seq": lax.rem(seq + by, blocks)})
    taps_load = load(taps_hbm, taps, False)
    proj_loads[0] = load(proj_hbm.at[0], proj.at[0], False)
    table_loads = [
        load(first_hbm, first, False),
        load(ahead_hbm, ahead, False),
        load(back_hbm, back, False),
        load(last_hbm, last, False),
        load(turn_hbm, turn, False),
    ]

    def load_rest():
        for copy in loads[4:]:
            copy.start()

    def remote(src, dst, send, recv, device):
        return pltpu.make_async_remote_copy(
            src_ref=src, dst_ref=dst, send_sem=send, recv_sem=recv,
            device_id=device, device_id_type=pl.DeviceIdType.MESH,
        )

    def hops(step):
        return sum(min(by, side - by) for by in divmod(step, side))

    peers = [
        lax.rem(z + step // side, side) * side + lax.rem(x + step % side, side)
        for step in sorted(range(1, side * side), key=hops, reverse=True)
    ]

    def exchange(src, dst, send, recv):
        pltpu.make_async_copy(src(seq), dst(seq), recv).start()

        for peer in peers:
            remote(src(peer), dst(seq), send, recv, {"seq": peer}).start()

    def exchange_arrived(src, dst, recv):
        pltpu.make_async_copy(src, dst, recv).wait()

    def exchange_left(src, dst, send, count):
        pltpu.make_async_copy(src.at[pl.ds(0, count)], dst.at[pl.ds(0, count)], send).wait()

    def rows_of(ref):
        return lambda peer: ref.at[pl.ds(pl.multiple_of(peer * 16, 16), 16)]

    def spread(block, part):
        for tile in range(HALF // COLS):
            relay[pl.ds((part * (HALF // COLS) + tile) * 16, 16), :] = block[
                :, tile * COLS : (tile + 1) * COLS
            ]

    def turn_weights(kind):
        proj_loads[kind].wait()
        for ahead_by in range(4):
            lane = pl.multiple_of(lax.rem(y + ahead_by, 4) * 128, 128)
            turned = proj[kind, :, pl.ds(lane, 128)].T
            for side in range(2):
                place = (1 - core if side == 0 else core) * 128 + 32 * ahead_by
                if kind == 0:
                    for part in range(2):
                        row = pl.multiple_of(place, 32)
                        weights[MIXES + part, pl.ds(row, 32), :] = turned[
                            side * 64 + 32 * part : side * 64 + 32 * part + 32
                        ]
                else:
                    for part in range(MIXES):
                        row = pl.multiple_of(place + 16 * (kind - 1), 16)
                        weights[part, pl.ds(row, 16), :] = turned[
                            side * 64 + 16 * part : side * 64 + 16 * part + 16
                        ]

    pieces = ((2, 0), (2, 1), (1, 1), (3, 0), (1, 0), (3, 1), (0, 0), (0, 1))
    def groups(c):
        return ((0, 2), (2, 2), (4, 4)) if c == 0 else ((0, 8),)

    def core_copy(c, group):
        part = pl.ds(*groups(c)[group])
        return remote(
            core_out.at[c, part], core_in.at[c, part], core_send.at[c, group],
            core_recv.at[c, group], partner,
        )

    def summed(c, piece):
        return own[c, piece] + core_in[c, piece].astype(F32)

    def ring_copy(c, kind):
        return remote(
            ring_out.at[c, kind], ring_in.at[c, kind], ring_send.at[c, kind],
            ring_recv.at[c, kind], right if kind % 2 == 0 else left,
        )

    def multiply(c):
        for h in range(2):
            if c == 0:
                hidden_loads[h].wait()
            product = lax.dot_general(
                weights[c], hidden[h * HALF : (h + 1) * HALF],
                (((1,), (1,)), ((), ())), preferred_element_type=F32,
            )
            for piece, (owner, half) in enumerate(pieces):
                if half == h:
                    core_out[c, piece] = product[owner * 32 : owner * 32 + 32].astype(BF16)
                    own[c, piece] = product[128 + owner * 32 : 160 + owner * 32]

    def core_go(c):
        for group in range(len(groups(c))):
            core_copy(c, group).start()

    def send_pieces(c, group):
        if group < len(groups(c)):
            core_copy(c, group).wait_recv()
        for kind in (2 * group, 2 * group + 1):
            ring_out[c, kind] = summed(c, kind).astype(BF16)
            ring_copy(c, kind).start()

    def far(c):
        send_pieces(c, 0)

    def near(c):
        send_pieces(c, 1)

    def pass_on(c):
        if c == 0:
            core_copy(c, 2).wait_recv()
        for h in range(2):
            ring_copy(c, h).wait_recv()
            ring_out[c, 4 + h] = (summed(c, 4 + h) + ring_in[c, h].astype(F32)).astype(BF16)
            ring_copy(c, 4 + h).start()

    def finish(c):
        for h in range(2):
            total = summed(c, 6 + h)
            for kind in (3, 4) if h == 0 else (2, 5):
                ring_copy(c, kind).wait_recv()
                total = total + ring_in[c, kind].astype(F32)
            if c >= MIXES:
                gates[pl.ds((c - MIXES) * 32, 32), pl.ds(h * HALF, HALF)] = total
            else:
                spread(total[:16] * total[16:], h)
        if c < MIXES:
            for peer in range(16):
                mixed_out[c, peer * 16 : peer * 16 + 16] = relay[
                    pl.ds(peer, 16, stride=16), :
                ].astype(BF16)
            exchange(
                rows_of(mixed_out.at[c]), rows_of(mixed_in.at[c]), mixed_send.at[c],
                mixed_recv.at[c],
            )

    def transformed(signals):
        wide = jnp.concatenate(signals, axis=1)
        value = dot(first[0], wide) + dot(first[1], wide)
        parts = []
        for n in range(len(signals)):
            real = value[:ROWS, n * COLS : (n + 1) * COLS]
            imag = value[ROWS:, n * COLS : (n + 1) * COLS]
            parts.append(
                jnp.concatenate(
                    [real * turn[0] - imag * turn[1], real * turn[1] + imag * turn[0]], axis=1
                )
            )
        high, low = halves_of(jnp.concatenate(parts, axis=0))
        return dot(high, ahead[0]) + dot(high, ahead[1]) + dot(low, ahead[0])

    def arrange_taps():
        taps_load.wait()
        for q in range(MIXES):
            for h in range(2):
                spread(taps[q * 16 : q * 16 + 16, h * HALF : (h + 1) * HALF].astype(F32), h)
            for peer in range(16):
                taps_out[peer, q] = relay[pl.ds(peer, 16, stride=16), :].astype(BF16)

    def send_taps():
        exchange(lambda peer: taps_out.at[peer], lambda peer: taps_in.at[peer], taps_send, taps_recv)

    def filter_spectra():
        exchange_arrived(taps_out, taps_in, taps_recv)
        for copy in table_loads:
            copy.wait()
        value = transformed([taps_in[:, q].reshape(ROWS, COLS) for q in range(MIXES)])
        spectrum[...] = value.reshape(MIXES, ROWS, 2 * COLS)

    def convolve(q):
        exchange_arrived(mixed_out.at[q], mixed_in.at[q], mixed_recv.at[q])
        value = transformed([mixed_in[q]])
        real, imag = value[:, :COLS], value[:, COLS:]
        freal, fimag = spectrum[q, :, :COLS], spectrum[q, :, COLS:]
        value = jnp.concatenate(
            [real * freal - imag * fimag, real * fimag + imag * freal], axis=1
        )
        high, low = halves_of(value)
        value = dot(high, back[0]) + dot(high, back[1]) + dot(low, back[0])
        real, imag = value[:, :COLS], value[:, COLS:]
        value = jnp.concatenate(
            [real * turn[0] + imag * turn[1], imag * turn[0] - real * turn[1]], axis=0
        )
        high, low = halves_of(value)
        value = dot(last[0], high) + dot(last[0], low) + dot(last[1], high)
        conv_out[q] = value.astype(BF16)
        exchange(rows_of(conv_out.at[q]), rows_of(conv_in.at[q]), conv_send.at[q], conv_recv.at[q])

    def emit(q):
        exchange_arrived(conv_out.at[q], conv_in.at[q], conv_recv.at[q])
        rows = pl.ds(q * 16, 16)
        relay[...] = conv_in[q].astype(F32)
        for tile in range(16):
            lanes = pl.ds(tile * COLS, COLS)
            part = relay[pl.ds(tile, 16, stride=16), :]
            gated[rows, lanes] = (gates[rows, lanes] * part).astype(BF16)
        pltpu.make_async_copy(gated.at[rows], out_hbm.at[rows], store_sem.at[q]).start()

    turn_weights(1)
    turn_weights(2)
    multiply(0)
    pl.semaphore_wait(barrier, 18)
    core_go(0)
    load_rest()
    multiply(1)
    core_go(1)
    far(0)
    near(0)
    multiply(2)
    core_go(2)
    arrange_taps()
    send_taps()
    far(1)
    turn_weights(0)
    multiply(3)
    core_go(3)
    pass_on(0)
    near(1)
    far(2)
    multiply(4)
    core_go(4)
    pass_on(1)
    near(2)
    far(3)
    multiply(5)
    core_go(5)
    filter_spectra()
    finish(0)
    pass_on(2)
    near(3)
    finish(1)
    pass_on(3)
    far(4)
    near(4)
    far(5)
    near(5)
    convolve(0)
    finish(2)
    finish(3)
    convolve(1)
    pass_on(4)
    convolve(2)
    pass_on(5)
    convolve(3)
    finish(4)
    emit(0)
    emit(1)
    finish(5)
    emit(2)
    emit(3)

    for c in range(CHUNKS):
        for group in range(len(groups(c))):
            core_copy(c, group).wait_send()
        for kind in range(6):
            ring_copy(c, kind).wait_send()
    exchange_left(taps_out, taps_in, taps_send, blocks - 1)
    for q in range(MIXES):
        exchange_left(mixed_out.at[q], mixed_in.at[q], mixed_send.at[q], (blocks - 1) * 16)
        exchange_left(conv_out.at[q], conv_in.at[q], conv_send.at[q], (blocks - 1) * 16)
        rows = pl.ds(q * 16, 16)
        pltpu.make_async_copy(gated.at[rows], out_hbm.at[rows], store_sem.at[q]).wait()


def per_device(hidden_in, projection, filter_taps):
    tables = transform_tables()
    blocks = lax.axis_size("seq")
    anywhere = pl.BlockSpec(memory_space=pl.ANY)
    dma = pltpu.SemaphoreType.DMA
    return pl.pallas_call(
        kernel,
        out_shape=jax.ShapeDtypeStruct(filter_taps.shape, BF16),
        in_specs=[anywhere] * (3 + len(tables)),
        out_specs=anywhere,
        scratch_shapes=[
            pltpu.VMEM(hidden_in.shape, BF16),
            pltpu.VMEM(projection.shape, BF16),
            pltpu.VMEM(filter_taps.shape, BF16),
        ]
        + [pltpu.VMEM(table.shape, table.dtype) for table in tables]
        + [
            pltpu.VMEM((CHUNKS, 256, hidden_in.shape[1]), BF16),
            pltpu.VMEM((CHUNKS, 8, 32, HALF), F32),
            pltpu.VMEM((CHUNKS, 8, 32, HALF), BF16),
            pltpu.VMEM((CHUNKS, 8, 32, HALF), BF16),
            pltpu.VMEM((CHUNKS, 6, 32, HALF), BF16),
            pltpu.VMEM((CHUNKS, 6, 32, HALF), BF16),
            pltpu.VMEM((256, COLS), F32),
            pltpu.VMEM((blocks, MIXES, 16, COLS), BF16),
            pltpu.VMEM((blocks, MIXES, 16, COLS), BF16),
            pltpu.VMEM((MIXES, ROWS, COLS), BF16),
            pltpu.VMEM((MIXES, ROWS, COLS), BF16),
            pltpu.VMEM((MIXES, ROWS, 2 * COLS), F32),
            pltpu.VMEM((MIXES, ROWS, COLS), BF16),
            pltpu.VMEM((MIXES, ROWS, COLS), BF16),
            pltpu.VMEM(filter_taps.shape, F32),
            pltpu.VMEM(filter_taps.shape, BF16),
            dma((11,)),
            dma((CHUNKS, 3)),
            dma((CHUNKS, 3)),
            dma((CHUNKS, 6)),
            dma((CHUNKS, 6)),
            dma(()),
            dma(()),
            dma((MIXES,)),
            dma((MIXES,)),
            dma((MIXES,)),
            dma((MIXES,)),
            dma((MIXES,)),
        ],
        compiler_params=pltpu.CompilerParams(
            collective_id=0, has_side_effects=True, vmem_limit_bytes=60 * 1024 * 1024
        ),
        cost_estimate=pl.CostEstimate(
            flops=7_000_000_000, bytes_accessed=8_000_000, transcendentals=0
        ),
    )(hidden_in, projection, filter_taps, *[jnp.asarray(table) for table in tables])


def solution(mesh):
    placed = (P("seq", "chan"), P(None, "chan", None), P("chan", "seq"))
    return jax.shard_map(
        per_device, mesh=mesh, in_specs=placed, out_specs=P("chan", "seq"), check_vma=False
    )
```
